128 devices in a mesh: dp: 8 (over x_lo, z), tensor: 16 (over x_hi, y, core).
Axes of the slice: x: 4 (x_hi: 2, x_lo: 2; x = x_hi * 2 + x_lo), y: 4, z: 4, core: 2. Of those that a mesh axis runs over, the one named last changes fastest.
Arguments:
- tokens: bfloat16 [4096, 4096], P(('dp', 'tensor')), may hold values from -6 to 6
- w_in: bfloat16 [4096, 16384], P('dp', 'tensor'), may hold values from -0.09375 to 0.09375
- w_out: bfloat16 [16384, 4096], P('tensor', 'dp'), may hold values from -0.046875 to 0.046875
- out_grad: bfloat16 [4096, 4096], P(('dp', 'tensor')), may hold values from -6 to 6
Outputs:
- layer_out: bfloat16 [4096, 4096], P(('dp', 'tensor'))
- in_grad: bfloat16 [4096, 4096], P(('dp', 'tensor'))
- w_in_grad: float32 [4096, 16384], P('dp', 'tensor')
- w_out_grad: float32 [16384, 4096], P('tensor', 'dp')
The draws below stay inside these ranges and needn't reach their ends.
All inputs are finite; a program needn't handle non-finite values.
Results may differ from the reference program's by a relative error of at most 0.019.
Values may be sent and summed in bfloat16 or wider, within the bound.
No kernel may reach another device: no remote copies, remote signals or barrier semaphores. Data moves between devices by JAX's collectives and lax.ppermute only.
A program may use at most 256 MiB of HBM per device.

```python
import math
import jax
import jax.numpy as jnp
from jax import lax

D = 4096
FF = 16384
GROUP_TOK = 512
TOKENS = 4096
N_DP = 8


def shard_levels(rng, shape, shards, least, largest):
    level = 1.0
    for position, blocks in shards:
        draws = jax.random.uniform(jax.random.fold_in(jax.random.fold_in(rng, 6), position), (blocks,), jnp.float32, least / len(shards), largest / len(shards))
        level = level * jnp.repeat(jnp.exp(draws), shape[position] // blocks).reshape((-1,) + (1,) * (len(shape) - 1 - position))
    return level


def normal_values(rng, dims, width, limit, split=(), kind=jnp.bfloat16):
    result = width * jax.random.normal(rng, dims, jnp.float32)
    if split:
        result = result * shard_levels(rng, dims, split, -0.22, 0.18)
    return jnp.clip(result, -limit, limit).astype(kind)


def setup_inputs(seed: int = 0) -> dict:
    splits = jax.random.split(jax.random.key(seed), 5)
    return {
        "tokens": normal_values(splits[0], (TOKENS, D), 1.0, 6.0, ((0, 128),)),
        "w_in": normal_values(splits[1], (D, FF), D ** -0.5, 0.09375, ((0, 8), (1, 16))),
        "w_out": normal_values(splits[2], (FF, D), FF ** -0.5, 0.046875, ((0, 16), (1, 8))),
        "out_grad": normal_values(splits[3], (TOKENS, D), 1.0, 6.0, ((0, 128),)),
    }


def gelu_exact(value):
    return 0.5 * value * (1.0 + lax.erf(value / math.sqrt(2.0)))

def gelu_slope(value):
    return 0.5 * (1.0 + lax.erf(value / math.sqrt(2.0))) + value * jnp.exp(-0.5 * value * value) / math.sqrt(2.0 * math.pi)

def reference(tokens, w_in, w_out, out_grad):
    preact = jnp.dot(tokens, w_in, preferred_element_type=jnp.float32)
    hidden = gelu_exact(preact).astype(jnp.bfloat16)
    layer_out = jnp.dot(hidden, w_out, preferred_element_type=jnp.float32).astype(jnp.bfloat16)
    hidden_grad = jnp.dot(out_grad, w_out.T, preferred_element_type=jnp.float32)
    preact_grad = (hidden_grad * gelu_slope(preact)).astype(jnp.bfloat16)
    in_grad = jnp.dot(preact_grad, w_in.T, preferred_element_type=jnp.float32).astype(jnp.bfloat16)
    grad_scale = 1.0 / math.sqrt(TOKENS)
    token_groups = tokens.reshape(N_DP, GROUP_TOK, D)
    preact_groups = preact_grad.reshape(N_DP, GROUP_TOK, FF)
    hidden_groups = hidden.reshape(N_DP, GROUP_TOK, FF)
    cotan_groups = out_grad.reshape(N_DP, GROUP_TOK, D)

    def one_group(carry, pieces):
        token_rows, preact_rows, hidden_rows, cotan_rows = pieces
        in_part = (jnp.dot(token_rows.T, preact_rows, preferred_element_type=jnp.float32) * grad_scale).astype(jnp.bfloat16)
        out_part = (jnp.dot(hidden_rows.T, cotan_rows, preferred_element_type=jnp.float32) * grad_scale).astype(jnp.bfloat16)
        in_part, out_part = lax.optimization_barrier((in_part, out_part))
        return ((carry[0] + in_part.astype(jnp.float32), carry[1] + out_part.astype(jnp.float32)), None)
    start_sums = (jnp.zeros((D, FF), jnp.float32), jnp.zeros((FF, D), jnp.float32))
    sums, unused = lax.scan(one_group, start_sums, (token_groups, preact_groups, hidden_groups, cotan_groups))
    return (layer_out, in_grad, sums[0], sums[1])
```

```python
import math

import jax
import jax.numpy as jnp
from jax import lax
from jax.sharding import PartitionSpec as P

AXES = ("dp", "tensor")
F32, BF16 = jnp.float32, jnp.bfloat16


def index_of(x, y, z, core):
    return ((x % 2 * 4 + z) * 2 + x // 2) * 8 + y * 2 + core


def route(step):
    pairs = []
    for x in range(4):
        for y in range(4):
            for z in range(4):
                for core in range(2):
                    tx, ty, tz, tc = step(x, y, z, core)
                    pairs.append((index_of(x, y, z, core), index_of(tx % 4, ty % 4, tz % 4, tc)))
    return pairs


def way(core):
    return 1 - 2 * core


AHEAD = {
    "x": route(lambda x, y, z, c: (x + way(c), y, z, c)),
    "y": route(lambda x, y, z, c: (x, y + way(c), z, c)),
    "z": route(lambda x, y, z, c: (x, y, z + way(c), c)),
}
BACK = {
    "x": route(lambda x, y, z, c: (x - way(c), y, z, c)),
    "y": route(lambda x, y, z, c: (x, y - way(c), z, c)),
    "z": route(lambda x, y, z, c: (x, y, z - way(c), c)),
}
PAIR = route(lambda x, y, z, c: (x ^ 1, y, z, c))
SWAP = route(lambda x, y, z, c: (x, y, z, 1 - c))


def send(value, pairs):
    return lax.ppermute(value, AXES, pairs)


def ring_gather(axis, own):
    behind = send(own, AHEAD[axis])
    ahead = send(own, BACK[axis])
    return [own, behind, ahead, send(behind, AHEAD[axis])]


def ring_scatter(axis, parts):
    through = send(parts[3], BACK[axis])
    near = send(parts[2], AHEAD[axis])
    far = send(add(parts[1], through), BACK[axis])
    return parts[0].astype(F32) + near.astype(F32) + far.astype(F32)


def add(left, right):
    return (left.astype(F32) + right.astype(F32)).astype(BF16)


def gelu_and_slope(value):
    cdf = 0.5 * (1.0 + lax.erf(value / math.sqrt(2.0)))
    slope = cdf + value * jnp.exp(-0.5 * value * value) / math.sqrt(2.0 * math.pi)
    return value * cdf, slope


def dot(left, right, dims):
    return lax.dot_general(left, right, (dims, ((), ())), preferred_element_type=F32)


def local(tokens, w_in, w_out, out_grad):
    dp, tensor = lax.axis_index("dp"), lax.axis_index("tensor")
    x_lo, z, core = dp // 4, dp % 4, tensor % 2
    side = 1 - 2 * core
    rows, width = tokens.shape
    depth, units = w_in.shape[0], w_in.shape[1] // 2
    grad_scale = 1.0 / math.sqrt(rows * 128)

    def halves(value, axis):
        mine = lax.dynamic_slice_in_dim(value, x_lo * units, units, axis)
        other = lax.dynamic_slice_in_dim(value, (1 - x_lo) * units, units, axis)
        return mine, send(other, PAIR)

    in_mine, in_pair = halves(w_in, 1)
    in_blocks = [ring_gather("z", in_mine), ring_gather("z", in_pair)]
    out_mine, out_pair = halves(w_out, 0)
    out_blocks = ring_gather("z", jnp.stack([out_mine, out_pair]))

    both = jnp.stack([tokens, out_grad])
    half = width // 2
    left = ring_gather("x", jnp.stack(ring_gather("y", both[:, :, :half])))
    right = ring_gather("y", jnp.stack(ring_gather("x", both[:, :, half:])))
    left = [left, [send(v, SWAP) for v in left]]
    right = [right, [send(v, SWAP) for v in right]]

    def whole(which):
        lefts = jnp.stack([jnp.stack([v[:, which] for v in part]) for part in left])
        rights = jnp.stack([jnp.stack([v[:, which] for v in part], 1) for part in right])
        return jnp.concatenate([lefts, rights], -1).reshape(32 * rows, width)

    token_rows, cotan_rows = whole(0), whole(1)

    def place(b):
        offset = (z - b) * side % 4
        return jnp.where(offset == 2, 3, jnp.where(offset == 3, 2, offset))

    def ordered(stacked):
        return [
            lax.dynamic_index_in_dim(
                lax.dynamic_index_in_dim(stacked, x_lo ^ a, 0, False), place(b), 0, False
            )
            for a in range(2)
            for b in range(4)
        ]

    w_in_full = jnp.concatenate(ordered(jnp.stack([jnp.stack(v) for v in in_blocks])), 0)
    w_out_full = jnp.concatenate(ordered(jnp.stack(out_blocks, 1)), 1)

    preact = dot(token_rows, w_in_full, ((1,), (0,)))
    hidden, slope = gelu_and_slope(preact)
    hidden = hidden.astype(BF16)
    out_part = (dot(hidden, cotan_rows, ((0,), (0,))) * grad_scale).astype(BF16)
    layer_part = dot(hidden, w_out_full, ((1,), (0,))).astype(BF16)
    preact_grad = (dot(cotan_rows, w_out_full, ((1,), (1,))) * slope).astype(BF16)
    in_part = (dot(token_rows, preact_grad, ((0,), (0,))) * grad_scale).astype(BF16)
    in_grad_part = dot(preact_grad, w_in_full, ((1,), (1,))).astype(BF16)

    def weight_sum(part, axis):
        shape = (2, 4, depth, units) if axis == 0 else (units, 2, 4, depth)
        blocks = part.reshape(shape)
        if axis:
            blocks = blocks.transpose(1, 2, 0, 3)
        mine = lax.dynamic_index_in_dim(blocks, x_lo, 0, False)
        pair = lax.dynamic_index_in_dim(blocks, 1 - x_lo, 0, False)
        blocks = jnp.stack([mine, pair])
        offsets = [z, (z - side) % 4, (z + side) % 4, (z + 2) % 4]
        parts = [lax.dynamic_index_in_dim(blocks, o, 1, False) for o in offsets]
        total = ring_scatter("z", parts)
        here = total[0]
        there = send(total[1].astype(BF16), PAIR).astype(F32)
        first = jnp.where(x_lo == 0, here, there)
        second = jnp.where(x_lo == 0, there, here)
        return jnp.concatenate([first, second], 1 - axis)

    def row_sum(part):
        part = part.reshape(2, 16 * rows, width)
        part = add(part[0], send(part[1], SWAP)).reshape(4, 4, rows, width)
        lefts = ring_scatter("x", [part[i, :, :, :half] for i in range(4)]).astype(BF16)
        lefts = ring_scatter("y", [lefts[i] for i in range(4)])
        rights = ring_scatter("y", [part[:, i, :, half:] for i in range(4)]).astype(BF16)
        rights = ring_scatter("x", [rights[i] for i in range(4)])
        return jnp.concatenate([lefts, rights], -1).astype(BF16)

    return (
        row_sum(layer_part),
        row_sum(in_grad_part),
        weight_sum(in_part, 0),
        weight_sum(out_part, 1),
    )


def solution(mesh):
    return jax.shard_map(
        local,
        mesh=mesh,
        in_specs=(
            P(("dp", "tensor"), None),
            P("dp", "tensor"),
            P("tensor", "dp"),
            P(("dp", "tensor"), None),
        ),
        out_specs=(
            P(("dp", "tensor"), None),
            P(("dp", "tensor"), None),
            P("dp", "tensor"),
            P("tensor", "dp"),
        ),
        check_vma=False,
    )
```

```python
import functools
import math

import jax
import jax.numpy as jnp
from jax import lax
from jax.experimental import pallas as pl
from jax.experimental.pallas import tpu as pltpu
from jax.sharding import PartitionSpec as P

AXES = ("dp", "tensor")
F32, BF16 = jnp.float32, jnp.bfloat16
TILE = 512


def index_of(x, y, z, core):
    return ((x % 2 * 4 + z) * 2 + x // 2) * 8 + y * 2 + core


def route(step):
    pairs = []
    for x in range(4):
        for y in range(4):
            for z in range(4):
                for core in range(2):
                    tx, ty, tz, tc = step(x, y, z, core)
                    pairs.append((index_of(x, y, z, core), index_of(tx % 4, ty % 4, tz % 4, tc)))
    return pairs


def way(core):
    return 1 - 2 * core


def along(hop, first):
    return route(lambda x, y, z, c: (x + hop, y, z, c) if c == first else (x, y + hop, z, c))


Z_AHEAD = route(lambda x, y, z, c: (x, y, z + way(c), c))
Z_BACK = route(lambda x, y, z, c: (x, y, z - way(c), c))
LONG_UP, LONG_DOWN = along(1, 0), along(-1, 0)
SHORT_UP, SHORT_DOWN, SHORT_FAR = along(1, 1), along(-1, 1), along(2, 1)
PAIR = route(lambda x, y, z, c: (x ^ 1, y, z, c))
SWAP = route(lambda x, y, z, c: (x, y, z, 1 - c))


def send(value, pairs):
    return lax.ppermute(value, AXES, pairs)


def after(value, *others):
    return lax.optimization_barrier((value, others))[0]


def add(*terms):
    return sum(t.astype(F32) for t in terms)


def gelu_and_slope(value):
    cdf = 0.5 * (1.0 + lax.erf(value / math.sqrt(2.0)))
    slope = cdf + value * jnp.exp(-0.5 * value * value) / math.sqrt(2.0 * math.pi)
    return value * cdf, slope


def dot(left, right, dims):
    return lax.dot_general(left, right, (dims, ((), ())), preferred_element_type=F32)


def params():
    return pltpu.CompilerParams(vmem_limit_bytes=14 << 20)


def cost(rows, depth, columns):
    return pl.CostEstimate(
        flops=2 * rows * depth * columns,
        bytes_accessed=2 * (rows * depth + depth * columns + rows * columns),
        transcendentals=0,
    )


def weight_part_body(scale, table, left, right, *rest):
    total = dot(left[...], right[...], ((0,), (0,))) * scale
    for term in rest[:-1]:
        total += term[...].reshape(total.shape).astype(F32)
    rest[-1][...] = total.astype(rest[-1].dtype).reshape(rest[-1].shape)


def weight_part(table, left, right, pick, first, count, scale, kind, *terms):
    rows = left.shape[0]
    whole = pl.BlockSpec((rows, TILE), lambda j, t: (0, 0))
    block = pl.BlockSpec((rows, TILE), lambda j, t: (0, t[first + j]))
    tile = pl.BlockSpec((1, TILE, TILE), lambda j, t: (j, 0, 0))
    return pl.pallas_call(
        functools.partial(weight_part_body, scale),
        grid_spec=pltpu.PrefetchScalarGridSpec(
            num_scalar_prefetch=1,
            grid=(count,),
            in_specs=[block, whole][:: 1 if pick == 0 else -1] + [tile] * len(terms),
            out_specs=tile,
        ),
        out_shape=jax.ShapeDtypeStruct((count, TILE, TILE), kind),
        compiler_params=params(),
        cost_estimate=cost(TILE, rows, count * TILE),
    )(table, left, right, *terms)


def row_part_body(dims, left, right, *rest):
    total = dot(left[...], right[...], dims)
    outs = rest
    if len(rest) == 5:
        total += rest[0][...].astype(F32)
        outs = rest[1:]
    size = total.shape[0] // len(outs)
    for i, out in enumerate(outs):
        out[...] = total[i * size : (i + 1) * size].astype(BF16)


def row_part(left, right, half, axis, *terms):
    rows, width = left.shape[0] // 2, right.shape[axis]
    tile = pl.BlockSpec((rows, TILE), lambda n: (0, n))
    parts = 4 if terms else 1
    out = pl.BlockSpec((rows // parts, TILE), lambda n: (0, n))
    weight = pl.BlockSpec((TILE, TILE), (lambda n: (0, n)) if axis else (lambda n: (n, 0)))
    return pl.pallas_call(
        functools.partial(row_part_body, ((1,), (1 - axis,))),
        grid=(width // TILE,),
        in_specs=[pl.BlockSpec((rows, TILE), lambda n: (half, 0)), weight] + [tile] * len(terms),
        out_specs=[out] * parts,
        out_shape=[jax.ShapeDtypeStruct((rows // parts, width), BF16)] * parts,
        compiler_params=params(),
        cost_estimate=cost(rows, TILE, width),
    )(left, right, *terms)


def local(tokens, w_in, w_out, out_grad):
    dp, tensor = lax.axis_index("dp"), lax.axis_index("tensor")
    x_lo, z, core = dp // 4, dp % 4, tensor % 2
    side = 1 - 2 * core
    rows = tokens.shape[0]
    grad_scale = 1.0 / math.sqrt(rows * 128)

    ring = [z, (z - side) % 4, (z + side) % 4, (z + 2) % 4]
    places = [a * 4 + b for a in (x_lo, 1 - x_lo) for b in ring]
    table = jnp.stack(places).astype(jnp.int32)
    part_table = table.reshape(2, 4).T.reshape(8)

    def halves(value, axis):
        mine = lax.dynamic_slice_in_dim(value, x_lo * TILE, TILE, axis)
        other = lax.dynamic_slice_in_dim(value, (1 - x_lo) * TILE, TILE, axis)
        return mine, other

    in_mine, in_other = halves(w_in, 1)
    out_mine, out_other = halves(w_out, 0)
    both = jnp.stack(after((tokens, out_grad), in_mine))

    in_a_behind, in_a_ahead = send(in_mine, Z_AHEAD), send(in_mine, Z_BACK)
    short_up, short_down, short_far = send(both, SHORT_UP), send(both, SHORT_DOWN), send(both, SHORT_FAR)
    in_a_far = send(in_a_behind, Z_AHEAD)
    out_a_behind = send(after(out_mine, in_a_ahead), Z_AHEAD)
    rows_own = jnp.concatenate([both, short_up, short_down, short_far], 1)
    rows_up, rows_down = send(rows_own, LONG_UP), send(rows_own, LONG_DOWN)
    in_pair = send(after(in_other, in_a_ahead, short_up), PAIR)
    out_a_ahead = send(after(out_mine, in_a_far, short_far), Z_BACK)
    in_b_behind = send(after(in_pair, out_a_behind), Z_AHEAD)
    out_pair = send(after(out_other, in_pair), PAIR)
    in_b_ahead = send(after(in_pair, out_a_ahead), Z_BACK)
    in_b_far = send(after(in_b_behind, out_pair), Z_AHEAD)
    out_a_far = send(after(out_a_behind, in_b_ahead), Z_AHEAD)
    tok_far = send(after(rows_up, out_pair)[0], LONG_UP)
    cot_far = send(after(rows_down, out_pair)[1], LONG_DOWN)
    out_b_behind = send(after(out_pair, in_b_far, rows_up, rows_down), Z_AHEAD)
    out_b_ahead = send(after(out_pair, out_a_far), Z_BACK)
    out_b_far = send(after(out_b_behind, tok_far, cot_far), Z_AHEAD)
    in_a = [in_mine, in_a_behind, in_a_ahead, in_a_far]
    in_b = [in_pair, in_b_behind, in_b_ahead, in_b_far]
    out_a = [out_mine, out_a_behind, out_a_ahead, out_a_far]
    out_b = [out_pair, out_b_behind, out_b_ahead, out_b_far]

    rows_own_swap = send(after(rows_own, rows_up), SWAP)
    rows_up_swap = send(after(rows_up, rows_own_swap), SWAP)
    rows_down_swap = send(after(rows_down, rows_up_swap), SWAP)

    def whole(which, far):
        near = [rows_own[which], rows_up[which], rows_down[which], far]
        swap = [rows_own_swap[which], rows_up_swap[which], rows_down_swap[which], send(far, SWAP)]
        return jnp.concatenate(near + swap, 0)

    token_rows, cotan_rows = whole(0, tok_far), whole(1, cot_far)

    def place(b):
        offset = (z - b) * side % 4
        return jnp.where(offset == 2, 3, jnp.where(offset == 3, 2, offset))

    def ordered(stacked):
        return [
            lax.dynamic_index_in_dim(
                lax.dynamic_index_in_dim(stacked, x_lo ^ a, 0, False), place(b), 0, False
            )
            for a in range(2)
            for b in range(4)
        ]

    w_in_full = jnp.concatenate(ordered(jnp.stack([jnp.stack(in_a), jnp.stack(in_b)])), 0)
    preact = dot(token_rows, w_in_full, ((1,), (0,)))
    hidden, slope = gelu_and_slope(preact)
    hidden = hidden.astype(BF16)

    out_piece = functools.partial(weight_part, part_table, hidden, cotan_rows, 1)
    out_opposite = out_piece(6, 2, grad_scale, BF16)
    out_through = send(out_opposite, Z_BACK)
    out_beside = out_piece(4, 2, grad_scale, BF16)
    out_near = send(out_beside, Z_AHEAD)
    out_b[3] = after(out_b_far, out_opposite, out_beside)
    out_ab = jnp.stack([jnp.stack(out_a), jnp.stack(out_b)])
    w_out_full = jnp.concatenate(ordered(out_ab), 1)
    (layer_other,) = row_part(hidden, w_out_full, 1, 1)
    layer_swap = send(layer_other, SWAP)
    hidden_grad = dot(after(cotan_rows, layer_other), w_out_full, ((1,), (1,)))
    preact_grad = (hidden_grad * slope).astype(BF16)
    out_third = weight_part(
        part_table, after(hidden, preact_grad), cotan_rows, 1, 2, 2, grad_scale, BF16, out_through
    )
    out_last = send(out_third, Z_BACK)
    layer = row_part(after(hidden, out_third), w_out_full, 0, 1, layer_swap)
    preact_grad = after(preact_grad, layer[0], out_near)
    (grads_other,) = row_part(preact_grad, w_in_full, 1, 0)
    preact_grad = after(preact_grad, grads_other)
    grads_swap = send(grads_other, SWAP)

    in_piece = functools.partial(weight_part, part_table, token_rows)
    in_opposite = [in_piece(preact_grad, 0, 6 + j, 1, grad_scale, BF16) for j in (1, 0)]
    in_through = [send(v, Z_BACK) for v in in_opposite]
    preact_grad = after(preact_grad, *in_opposite)
    grads = row_part(preact_grad, w_in_full, 0, 0, grads_swap)

    layer_through = send(layer[3], LONG_DOWN)
    layer_near = send(layer[2], LONG_UP)
    layer_third = add(layer[1], layer_through).astype(BF16)
    layer_far = send(layer_third, LONG_DOWN)
    grads_through = send(grads[3], LONG_UP)
    grads_near = send(grads[1], LONG_DOWN)
    grads_far = send(add(grads[2], grads_through).astype(BF16), LONG_UP)

    preact_grad = after(preact_grad, grads[0], layer_third, out_last)
    in_beside = [in_piece(preact_grad, 0, 4 + j, 1, grad_scale, BF16) for j in (1, 0)]
    in_near = [send(v, Z_AHEAD) for v in in_beside]
    in_last = [
        send(in_piece(preact_grad, 0, 2 + j, 1, grad_scale, BF16, v), Z_BACK)
        for j, v in zip((1, 0), in_through)
    ]
    out_sum = weight_part(
        part_table, after(hidden, *in_beside), cotan_rows, 1, 0, 2, grad_scale, F32, out_near, out_last
    )
    out_there = send(out_sum[1].astype(BF16), PAIR)
    in_there, in_here = [
        in_piece(preact_grad, 0, j, 1, grad_scale, kind, near, last)[0]
        for j, kind, near, last in zip((1, 0), (BF16, F32), in_near, in_last)
    ]
    in_there = send(in_there, PAIR)

    def beside(here, there, axis):
        there = there.astype(F32)
        return jnp.concatenate(
            [jnp.where(x_lo == 0, here, there), jnp.where(x_lo == 0, there, here)], axis
        )

    sums = jnp.stack([add(layer[0], layer_near, layer_far), add(grads[0], grads_near, grads_far)])
    sums = sums.reshape(2, 4, rows, -1)
    up = send(sums[:, 2].astype(BF16), SHORT_UP)
    down = send(sums[:, 1].astype(BF16), SHORT_DOWN)
    far = send(sums[:, 3].astype(BF16), SHORT_FAR)
    total = add(sums[:, 0], up, down, far).astype(BF16)

    return (
        total[0],
        total[1],
        beside(in_here, in_there, 1),
        beside(out_sum[0], out_there, 0),
    )


def solution(mesh):
    return jax.shard_map(
        local,
        mesh=mesh,
        in_specs=(
            P(("dp", "tensor"), None),
            P("dp", "tensor"),
            P("tensor", "dp"),
            P(("dp", "tensor"), None),
        ),
        out_specs=(
            P(("dp", "tensor"), None),
            P(("dp", "tensor"), None),
            P("dp", "tensor"),
            P("tensor", "dp"),
        ),
        check_vma=False,
    )
```

```python
import functools
import math

import jax
import jax.numpy as jnp
from jax import lax
from jax.experimental import pallas as pl
from jax.experimental.pallas import tpu as pltpu
from jax.sharding import PartitionSpec as P

AXES = ("dp", "tensor")
F32, BF16 = jnp.float32, jnp.bfloat16
TILE = 512


def index_of(x, y, z, core):
    return ((x % 2 * 4 + z) * 2 + x // 2) * 8 + y * 2 + core


def route(step):
    pairs = []
    for x in range(4):
        for y in range(4):
            for z in range(4):
                for core in range(2):
                    tx, ty, tz, tc = step(x, y, z, core)
                    pairs.append((index_of(x, y, z, core), index_of(tx % 4, ty % 4, tz % 4, tc)))
    return pairs


def way(core):
    return 1 - 2 * core


def along(hop, first):
    return route(lambda x, y, z, c: (x + hop, y, z, c) if c == first else (x, y + hop, z, c))


Z_AHEAD = route(lambda x, y, z, c: (x, y, z + way(c), c))
Z_BACK = route(lambda x, y, z, c: (x, y, z - way(c), c))
LONG_UP, LONG_DOWN = along(1, 0), along(-1, 0)
SHORT_UP, SHORT_DOWN, SHORT_FAR = along(1, 1), along(-1, 1), along(2, 1)
PAIR = route(lambda x, y, z, c: (x ^ 1, y, z, c))
Z_BACK_PAIR = route(lambda x, y, z, c: (x ^ 1, y, z - way(c), c))
SWAP = route(lambda x, y, z, c: (x, y, z, 1 - c))


def send(value, pairs):
    return lax.ppermute(value, AXES, pairs)


def after(value, *others):
    return lax.optimization_barrier((value, others))[0]


def marker_body(value, out):
    out[...] = value[...]


def marker(*others):
    return pl.pallas_call(
        marker_body,
        out_shape=jax.ShapeDtypeStruct((8, 128), F32),
        cost_estimate=pl.CostEstimate(flops=1, bytes_accessed=1, transcendentals=0),
    )(after(jnp.zeros((8, 128), F32), *others))


class Clock:
    def __init__(self):
        self.token, self.waits = jnp.zeros((8, 128), F32), ()

    def step(self, *waits):
        if self.waits is not None:
            self.token = marker(self.token, *self.waits)
        self.waits = waits

    def __call__(self, value):
        return after(value, self.token, *self.waits)


def add(*terms):
    return sum(t.astype(F32) for t in terms)


def gelu_and_slope(value):
    cdf = 0.5 * (1.0 + lax.erf(value / math.sqrt(2.0)))
    slope = cdf + value * jnp.exp(-0.5 * value * value) / math.sqrt(2.0 * math.pi)
    return value * cdf, slope


def dot(left, right, dims):
    return lax.dot_general(left, right, (dims, ((), ())), preferred_element_type=F32)


def params():
    return pltpu.CompilerParams(vmem_limit_bytes=14 << 20)


def cost(rows, depth, columns):
    return pl.CostEstimate(flops=1, bytes_accessed=1, transcendentals=0)


def weight_part_body(scale, table, left, right, *rest):
    total = dot(left[...], right[...], ((0,), (0,))) * scale
    for term in rest[:-1]:
        total += term[...].reshape(total.shape).astype(F32)
    rest[-1][...] = total.astype(rest[-1].dtype).reshape(rest[-1].shape)


def weight_part(table, left, right, pick, first, count, scale, kind, *terms):
    rows = left.shape[0]
    whole = pl.BlockSpec((rows, TILE), lambda j, t: (0, 0))
    block = pl.BlockSpec((rows, TILE), lambda j, t: (0, t[first + j]))
    tile = pl.BlockSpec((1, TILE, TILE), lambda j, t: (j, 0, 0))
    return pl.pallas_call(
        functools.partial(weight_part_body, scale),
        grid_spec=pltpu.PrefetchScalarGridSpec(
            num_scalar_prefetch=1,
            grid=(count,),
            in_specs=[block, whole][:: 1 if pick == 0 else -1] + [tile] * len(terms),
            out_specs=tile,
        ),
        out_shape=jax.ShapeDtypeStruct((count, TILE, TILE), kind),
        compiler_params=params(),
        cost_estimate=cost(TILE, rows, count * TILE),
    )(table, left, right, *terms)


def row_part_body(dims, left, right, other, *own):
    total = dot(left[...], right[...], dims)
    size = own[0].shape[0]
    for i, out in enumerate(own):
        out[...] = total[i * size : (i + 1) * size].astype(BF16)
    other[...] = total[len(own) * size :].astype(BF16)


def row_part(left, right, axis):
    rows, width, tile = left.shape[0], right.shape[axis], 2 * TILE
    weight = pl.BlockSpec((TILE, tile), lambda n: (0, n)) if axis else pl.BlockSpec((tile, TILE), lambda n: (n, 0))
    sizes = [rows // 2] + [rows // 8] * 4
    return pl.pallas_call(
        functools.partial(row_part_body, ((1,), (1 - axis,))),
        grid=(width // tile,),
        in_specs=[pl.BlockSpec((rows, TILE), lambda n: (0, 0)), weight],
        out_specs=[pl.BlockSpec((size, tile), lambda n: (0, n)) for size in sizes],
        out_shape=[jax.ShapeDtypeStruct((size, width), BF16) for size in sizes],
        compiler_params=pltpu.CompilerParams(vmem_limit_bytes=24 << 20),
        cost_estimate=cost(rows, TILE, width),
    )(left, right)


def preact_grad_body(left, right, slope, out, total):
    step = pl.program_id(0)
    product = dot(left[...], right[...], ((1,), (1,)))

    @pl.when(step == 0)
    def _():
        total[...] = product

    @pl.when(step > 0)
    def _():
        total[...] += product

    @pl.when(step == pl.num_programs(0) - 1)
    def _():
        out[...] = (total[...] * slope[...]).astype(BF16)


def preact_grad_of(left, right, slope):
    rows, width, tile = left.shape[0], left.shape[1], 2 * TILE
    whole = pl.BlockSpec((rows, TILE), lambda k: (0, 0))
    return pl.pallas_call(
        preact_grad_body,
        grid=(width // tile,),
        in_specs=[pl.BlockSpec((rows, tile), lambda k: (0, k)), pl.BlockSpec((TILE, tile), lambda k: (0, k)), whole],
        out_specs=whole,
        out_shape=jax.ShapeDtypeStruct((rows, TILE), BF16),
        scratch_shapes=[pltpu.VMEM((rows, TILE), F32)],
        compiler_params=pltpu.CompilerParams(vmem_limit_bytes=24 << 20),
        cost_estimate=cost(rows, TILE, width),
    )(left, right, slope)


def local(tokens, w_in, w_out, out_grad):
    dp, tensor = lax.axis_index("dp"), lax.axis_index("tensor")
    x_lo, z, core = dp // 4, dp % 4, tensor % 2
    side = 1 - 2 * core
    rows = tokens.shape[0]
    grad_scale = 1.0 / math.sqrt(rows * 128)

    ring = [z, (z - side) % 4, (z + side) % 4, (z + 2) % 4]
    places = [a * 4 + b for a in (x_lo, 1 - x_lo) for b in ring]
    table = jnp.stack(places).astype(jnp.int32)
    part_table = table.reshape(2, 4).T.reshape(8)

    def halves(value, axis):
        mine = lax.dynamic_slice_in_dim(value, x_lo * TILE, TILE, axis)
        other = lax.dynamic_slice_in_dim(value, (1 - x_lo) * TILE, TILE, axis)
        return mine, other

    in_mine, in_other = halves(w_in, 1)
    out_mine, out_other = halves(w_out, 0)
    both = jnp.stack([tokens, out_grad])

    clock = Clock()
    in_a_behind, in_a_ahead = send(in_mine, Z_AHEAD), send(in_mine, Z_BACK)
    in_pair = send(in_other, PAIR)
    clock.step()
    short_up, short_down = send(clock(both), SHORT_UP), send(clock(both), SHORT_DOWN)
    clock.step(in_a_behind, in_a_ahead)
    in_a_far = send(clock(in_a_behind), Z_AHEAD)
    short_far = send(clock(both), SHORT_FAR)
    clock.step(short_up, short_down, in_pair)
    start_in, start_out = clock(jnp.zeros((8 * TILE, TILE), BF16)), clock(jnp.zeros((TILE, 8 * TILE), BF16))
    in_pair = clock(in_pair)
    in_b_behind, in_b_ahead = send(in_pair, Z_AHEAD), send(in_pair, Z_BACK)
    clock.step(short_far, in_a_far)
    rows_own = clock(jnp.concatenate([both, short_up, short_down, short_far], 1))
    rows_up, rows_down = send(rows_own, LONG_UP), send(rows_own, LONG_DOWN)
    rows_own_swap = send(rows_own, SWAP)
    clock.step(rows_own_swap)
    out_pair = send(clock(out_other), PAIR)
    clock.step(in_b_behind, in_b_ahead)
    in_b_far = send(clock(in_b_behind), Z_AHEAD)
    clock.step(rows_up, rows_down, out_pair)
    rows_up, rows_down = clock(rows_up), clock(rows_down)
    tok_far, cot_far = send(rows_up[0], LONG_UP), send(rows_down[1], LONG_DOWN)
    rows_up_swap, rows_down_swap = send(rows_up, SWAP), send(rows_down, SWAP)
    out_own = jnp.stack([out_mine, clock(out_pair)])
    out_behind = send(out_own, Z_AHEAD)
    clock.step(rows_up_swap, rows_down_swap, in_b_far)
    out_ahead = send(clock(out_own), Z_BACK)
    clock.step(tok_far, cot_far, out_behind)
    tok_far_swap, cot_far_swap = send(clock(tok_far), SWAP), send(clock(cot_far), SWAP)
    out_far = send(clock(out_behind), Z_AHEAD)
    clock.step(tok_far_swap, cot_far_swap)

    in_full = start_in
    for i, piece in enumerate([in_mine, in_a_behind, in_a_ahead, in_a_far, in_pair, in_b_behind, in_b_ahead, in_b_far]):
        in_full = lax.dynamic_update_slice(in_full, piece, (places[i] * TILE, 0))
    out_full = start_out

    def placed(full, i, pieces):
        for j in range(2):
            full = lax.dynamic_update_slice(full, pieces[j], (0, places[i + 4 * j] * TILE))
        return full

    for i, pieces in enumerate((out_own, out_behind)):
        out_full = placed(out_full, i, pieces)
    def whole(which, far, far_swap):
        near = [rows_own[which], rows_up[which], rows_down[which], far]
        swap = [rows_own_swap[which], rows_up_swap[which], rows_down_swap[which], far_swap]
        return jnp.concatenate(near + swap, 0)

    token_rows = clock(whole(0, tok_far, tok_far_swap))
    cotan_rows = whole(1, cot_far, cot_far_swap)

    preact = dot(token_rows, in_full, ((1,), (0,)))
    hidden, slope = gelu_and_slope(preact)
    hidden = hidden.astype(BF16)


    def out_piece(*rest):
        return weight_part(part_table, clock(hidden), cotan_rows, 1, *rest)

    def in_piece(*rest):
        return weight_part(part_table, token_rows, clock(preact_grad), 0, *rest)

    clock.step(hidden)
    out_opposite = out_piece(6, 2, grad_scale, BF16)
    out_through = send(out_opposite, Z_BACK)
    out_beside = out_piece(4, 2, grad_scale, BF16)
    out_near = send(out_beside, Z_AHEAD)
    clock.step(out_ahead, out_opposite, out_beside)
    out_full = placed(out_full, 2, clock(out_ahead))
    clock.step(out_far, out_full)
    out_full = placed(clock(out_full), 3, clock(out_far))
    layer_other, *layer = row_part(clock(hidden), out_full, 1)
    clock.step(layer_other)
    layer_swap = send(clock(layer_other), SWAP)
    preact_grad = preact_grad_of(cotan_rows, clock(out_full), slope)
    clock.step(preact_grad, layer_swap)

    def parts(value):
        return [value[i : i + 4 * rows] for i in range(0, 16 * rows, 4 * rows)]

    layer = list(zip(layer, parts(clock(layer_swap))))
    layer_through = send(add(*layer[3]).astype(BF16), LONG_DOWN)
    layer_near = send(add(*layer[2]).astype(BF16), LONG_UP)
    in_opposite = in_piece(6, 2, grad_scale, BF16)
    grads_other, *grads = row_part(clock(preact_grad), in_full, 0)
    clock.step(in_opposite, grads_other, out_through, out_near, layer_through, layer_near)
    grads_swap = send(clock(grads_other), SWAP)
    in_through = send(clock(in_opposite), Z_BACK)
    layer_third = add(*layer[1], clock(layer_through)).astype(BF16)
    layer_far = send(layer_third, LONG_DOWN)
    out_third = out_piece(2, 2, grad_scale, BF16, clock(out_through))
    out_last = send(out_third, Z_BACK)
    clock.step(out_third, layer_third, grads_swap)
    grads = list(zip(grads, parts(clock(grads_swap))))
    grads_3, grads_1 = add(*grads[3]).astype(BF16), add(*grads[1]).astype(BF16)
    grads_through, grads_near = send(grads_3, LONG_UP), send(grads_1, LONG_DOWN)
    in_beside = [in_piece(4 + j, 1, grad_scale, BF16) for j in range(2)]
    clock.step(*in_beside, grads_1, grads_3, layer_far, in_through, out_last, grads_through, grads_near)
    in_near = [send(clock(v), Z_AHEAD) for v in in_beside]
    in_through = clock(in_through)
    in_third = [in_piece(2 + j, 1, grad_scale, BF16, in_through[j : j + 1]) for j in range(2)]
    in_last_1 = send(in_third[1], Z_BACK)
    grads_third = add(*grads[2], clock(grads_through)).astype(BF16)
    grads_far = send(grads_third, LONG_UP)
    out_sum = out_piece(0, 2, grad_scale, F32, out_near, out_last)
    out_there = send(out_sum[1].astype(BF16), PAIR)
    layer_sum = add(*layer[0], layer_near, clock(layer_far))
    clock.step(*in_third, layer_sum, grads_far, *in_near, in_last_1, out_there)
    in_last_0 = send(clock(in_third[0]), Z_BACK)
    in_there = in_piece(1, 1, grad_scale, BF16, clock(in_near[1]), clock(in_last_1))[0]
    in_there = send(in_there, PAIR)
    sums = jnp.stack([clock(layer_sum), add(*grads[0], grads_near, clock(grads_far))])

    def beside(here, there, axis):
        there = there.astype(F32)
        return jnp.concatenate(
            [jnp.where(x_lo == 0, here, there), jnp.where(x_lo == 0, there, here)], axis
        )

    sums = sums.reshape(2, 4, rows, -1)
    up = send(sums[:, 2].astype(BF16), SHORT_UP)
    down = send(sums[:, 1].astype(BF16), SHORT_DOWN)
    far = send(sums[:, 3].astype(BF16), SHORT_FAR)
    clock.step(up, down, far, in_last_0)
    in_here = in_piece(0, 1, grad_scale, F32, clock(in_near[0]), clock(in_last_0))[0]
    total = add(sums[:, 0], clock(up), clock(down), clock(far)).astype(BF16)

    return (
        total[0],
        total[1],
        beside(in_here, in_there, 1),
        beside(out_sum[0], out_there, 0),
    )


def solution(mesh):
    return jax.shard_map(
        local,
        mesh=mesh,
        in_specs=(
            P(("dp", "tensor"), None),
            P("dp", "tensor"),
            P("tensor", "dp"),
            P(("dp", "tensor"), None),
        ),
        out_specs=(
            P(("dp", "tensor"), None),
            P(("dp", "tensor"), None),
            P("dp", "tensor"),
            P("tensor", "dp"),
        ),
        check_vma=False,
    )
```

```python
import functools
import math

import jax
import jax.numpy as jnp
from jax import lax
from jax.experimental import pallas as pl
from jax.experimental.pallas import tpu as pltpu
from jax.sharding import PartitionSpec as P

AXES = ("dp", "tensor")
F32, BF16 = jnp.float32, jnp.bfloat16
TILE = 512


def index_of(x, y, z, core):
    return ((x % 2 * 4 + z) * 2 + x // 2) * 8 + y * 2 + core


def route(step):
    pairs = []
    for x in range(4):
        for y in range(4):
            for z in range(4):
                for core in range(2):
                    tx, ty, tz, tc = step(x, y, z, core)
                    pairs.append((index_of(x, y, z, core), index_of(tx % 4, ty % 4, tz % 4, tc)))
    return pairs


def way(core):
    return 1 - 2 * core


def along(hop, first):
    return route(lambda x, y, z, c: (x + hop, y, z, c) if c == first else (x, y + hop, z, c))


Z_AHEAD = route(lambda x, y, z, c: (x, y, z + way(c), c))
Z_BACK = route(lambda x, y, z, c: (x, y, z - way(c), c))
LONG_UP, LONG_DOWN = along(1, 0), along(-1, 0)
SHORT_UP, SHORT_DOWN, SHORT_FAR = along(1, 1), along(-1, 1), along(2, 1)
PAIR = route(lambda x, y, z, c: (x ^ 1, y, z, c))
Z_BACK_PAIR = route(lambda x, y, z, c: (x ^ 1, y, z - way(c), c))
SWAP = route(lambda x, y, z, c: (x, y, z, 1 - c))


def send(value, pairs):
    return lax.ppermute(value, AXES, pairs)


def after(value, *others):
    return lax.optimization_barrier((value, others))[0]


def marker_body(value, out):
    out[...] = value[...]


def marker(*others):
    return pl.pallas_call(
        marker_body,
        out_shape=jax.ShapeDtypeStruct((8, 128), F32),
        cost_estimate=pl.CostEstimate(flops=1, bytes_accessed=1, transcendentals=0),
    )(after(jnp.zeros((8, 128), F32), *others))


class Clock:
    def __init__(self):
        self.token, self.waits = jnp.zeros((8, 128), F32), ()

    def step(self, *waits):
        if self.waits is not None:
            self.token = marker(self.token, *self.waits)
        self.waits = waits

    def __call__(self, value):
        return after(value, self.token, *self.waits)


def add(*terms):
    return sum(t.astype(F32) for t in terms)


def gelu_and_slope(value):
    cdf = 0.5 * (1.0 + lax.erf(value / math.sqrt(2.0)))
    slope = cdf + value * jnp.exp(-0.5 * value * value) / math.sqrt(2.0 * math.pi)
    return value * cdf, slope


def dot(left, right, dims):
    return lax.dot_general(left, right, (dims, ((), ())), preferred_element_type=F32)


def params():
    return pltpu.CompilerParams(vmem_limit_bytes=14 << 20)


def cost(rows, depth, columns):
    return pl.CostEstimate(flops=1, bytes_accessed=1, transcendentals=0)


def weight_part_body(scale, table, left, right, *rest):
    total = dot(left[...], right[...], ((0,), (0,))) * scale
    for term in rest[:-1]:
        total += term[...].reshape(total.shape).astype(F32)
    rest[-1][...] = total.astype(rest[-1].dtype).reshape(rest[-1].shape)


def weight_part(table, left, right, pick, first, count, scale, kind, *terms):
    rows = left.shape[0]
    whole = pl.BlockSpec((rows, TILE), lambda j, t: (0, 0))
    block = pl.BlockSpec((rows, TILE), lambda j, t: (0, t[first + j]))
    tile = pl.BlockSpec((1, TILE, TILE), lambda j, t: (j, 0, 0))
    return pl.pallas_call(
        functools.partial(weight_part_body, scale),
        grid_spec=pltpu.PrefetchScalarGridSpec(
            num_scalar_prefetch=1,
            grid=(count,),
            in_specs=[block, whole][:: 1 if pick == 0 else -1] + [tile] * len(terms),
            out_specs=tile,
        ),
        out_shape=jax.ShapeDtypeStruct((count, TILE, TILE), kind),
        compiler_params=params(),
        cost_estimate=cost(TILE, rows, count * TILE),
    )(table, left, right, *terms)


def row_part_body(dims, left, right, other, *own):
    total = dot(left[...], right[...], dims)
    size = own[0].shape[0]
    for i, out in enumerate(own):
        out[...] = total[i * size : (i + 1) * size].astype(BF16)
    other[...] = total[len(own) * size :].astype(BF16)


def row_part(left, right, axis):
    rows, width, tile = left.shape[0], right.shape[axis], 2 * TILE
    weight = pl.BlockSpec((TILE, tile), lambda n: (0, n)) if axis else pl.BlockSpec((tile, TILE), lambda n: (n, 0))
    sizes = [rows // 2] + [rows // 8] * 4
    return pl.pallas_call(
        functools.partial(row_part_body, ((1,), (1 - axis,))),
        grid=(width // tile,),
        in_specs=[pl.BlockSpec((rows, TILE), lambda n: (0, 0)), weight],
        out_specs=[pl.BlockSpec((size, tile), lambda n: (0, n)) for size in sizes],
        out_shape=[jax.ShapeDtypeStruct((size, width), BF16) for size in sizes],
        compiler_params=pltpu.CompilerParams(vmem_limit_bytes=24 << 20),
        cost_estimate=cost(rows, TILE, width),
    )(left, right)


def preact_grad_body(left, right, slope, out, total):
    step = pl.program_id(0)
    product = dot(left[...], right[...], ((1,), (1,)))

    @pl.when(step == 0)
    def _():
        total[...] = product

    @pl.when(step > 0)
    def _():
        total[...] += product

    @pl.when(step == pl.num_programs(0) - 1)
    def _():
        out[...] = (total[...] * slope[...]).astype(BF16)


def preact_grad_of(left, right, slope):
    rows, width, tile = left.shape[0], left.shape[1], 2 * TILE
    whole = pl.BlockSpec((rows, TILE), lambda k: (0, 0))
    return pl.pallas_call(
        preact_grad_body,
        grid=(width // tile,),
        in_specs=[pl.BlockSpec((rows, tile), lambda k: (0, k)), pl.BlockSpec((TILE, tile), lambda k: (0, k)), whole],
        out_specs=whole,
        out_shape=jax.ShapeDtypeStruct((rows, TILE), BF16),
        scratch_shapes=[pltpu.VMEM((rows, TILE), F32)],
        compiler_params=pltpu.CompilerParams(vmem_limit_bytes=24 << 20),
        cost_estimate=cost(rows, TILE, width),
    )(left, right, slope)


def local(tokens, w_in, w_out, out_grad):
    dp, tensor = lax.axis_index("dp"), lax.axis_index("tensor")
    x_lo, z, core = dp // 4, dp % 4, tensor % 2
    side = 1 - 2 * core
    rows = tokens.shape[0]
    grad_scale = 1.0 / math.sqrt(rows * 128)

    ring = [z, (z - side) % 4, (z + side) % 4, (z + 2) % 4]
    places = [a * 4 + b for a in (x_lo, 1 - x_lo) for b in ring]
    table = jnp.stack(places).astype(jnp.int32)
    part_table = table.reshape(2, 4).T.reshape(8)

    def halves(value, axis):
        mine = lax.dynamic_slice_in_dim(value, x_lo * TILE, TILE, axis)
        other = lax.dynamic_slice_in_dim(value, (1 - x_lo) * TILE, TILE, axis)
        return mine, other

    in_mine, in_other = halves(w_in, 1)
    out_mine, out_other = halves(w_out, 0)
    both = jnp.stack([tokens, out_grad])

    clock = Clock()
    in_a_behind, in_a_ahead = send(in_mine, Z_AHEAD), send(in_mine, Z_BACK)
    pair = send(jnp.stack([in_other, out_other]), PAIR)
    clock.step()
    short_up, short_down = send(clock(both), SHORT_UP), send(clock(both), SHORT_DOWN)
    clock.step(in_a_behind, in_a_ahead)
    in_a_far = send(clock(in_a_behind), Z_AHEAD)
    short_far = send(clock(both), SHORT_FAR)
    clock.step(short_far, in_a_far, pair)
    in_pair, out_pair = clock(pair[0]), clock(pair[1])
    start_in, start_out = clock(jnp.zeros((8 * TILE, TILE), BF16)), clock(jnp.zeros((TILE, 8 * TILE), BF16))
    rows_own = clock(jnp.concatenate([both, short_up, short_down, short_far], 1))
    rows_up, rows_down = send(rows_own, LONG_UP), send(rows_own, LONG_DOWN)
    rows_own_swap = send(rows_own, SWAP)
    in_b_behind, in_b_ahead = send(in_pair, Z_AHEAD), send(in_pair, Z_BACK)
    clock.step(rows_own_swap)
    out_own = clock(jnp.stack([out_mine, out_pair]))
    clock.step(in_b_behind, in_b_ahead, out_own)
    in_b_far = send(clock(in_b_behind), Z_AHEAD)
    out_behind = send(clock(out_own), Z_AHEAD)
    clock.step(rows_up, rows_down, in_b_far, out_behind)
    rows_up, rows_down = clock(rows_up), clock(rows_down)
    tok_far, cot_far = send(rows_up[0], LONG_UP), send(rows_down[1], LONG_DOWN)
    rows_up_swap, rows_down_swap = send(rows_up, SWAP), send(rows_down, SWAP)
    out_ahead = send(clock(out_own), Z_BACK)
    clock.step(rows_up_swap, rows_down_swap)
    clock.step(tok_far, cot_far, out_ahead)
    tok_far_swap, cot_far_swap = send(clock(tok_far), SWAP), send(clock(cot_far), SWAP)
    out_far = send(clock(out_behind), Z_AHEAD)
    clock.step(tok_far_swap, cot_far_swap)

    in_full = start_in
    for i, piece in enumerate([in_mine, in_a_behind, in_a_ahead, in_a_far, in_pair, in_b_behind, in_b_ahead, in_b_far]):
        in_full = lax.dynamic_update_slice(in_full, piece, (places[i] * TILE, 0))
    out_full = start_out

    def placed(full, i, pieces):
        for j in range(2):
            full = lax.dynamic_update_slice(full, pieces[j], (0, places[i + 4 * j] * TILE))
        return full

    for i, pieces in enumerate((out_own, out_behind)):
        out_full = placed(out_full, i, pieces)
    def whole(which, far, far_swap):
        near = [rows_own[which], rows_up[which], rows_down[which], far]
        swap = [rows_own_swap[which], rows_up_swap[which], rows_down_swap[which], far_swap]
        return jnp.concatenate(near + swap, 0)

    token_rows = clock(whole(0, tok_far, tok_far_swap))
    cotan_rows = whole(1, cot_far, cot_far_swap)

    preact = dot(token_rows, in_full, ((1,), (0,)))
    hidden, slope = gelu_and_slope(preact)
    hidden = hidden.astype(BF16)


    def out_piece(*rest):
        return weight_part(part_table, clock(hidden), cotan_rows, 1, *rest)

    def in_piece(*rest):
        return weight_part(part_table, token_rows, clock(preact_grad), 0, *rest)

    clock.step(hidden)
    out_opposite = out_piece(6, 2, grad_scale, BF16)
    out_through = send(out_opposite, Z_BACK)
    out_beside = out_piece(4, 2, grad_scale, BF16)
    out_near = send(out_beside, Z_AHEAD)
    clock.step(out_ahead, out_opposite, out_beside)
    out_full = placed(out_full, 2, clock(out_ahead))
    clock.step(out_far, out_full)
    out_full = placed(clock(out_full), 3, clock(out_far))
    layer_other, *layer = row_part(clock(hidden), out_full, 1)
    clock.step(layer_other)
    layer_swap = send(clock(layer_other), SWAP)
    preact_grad = preact_grad_of(cotan_rows, clock(out_full), slope)
    clock.step(preact_grad, layer_swap)

    def parts(value):
        return [value[i : i + 4 * rows] for i in range(0, 16 * rows, 4 * rows)]

    layer = list(zip(layer, parts(clock(layer_swap))))
    layer_through = send(add(*layer[3]).astype(BF16), LONG_DOWN)
    layer_near = send(add(*layer[2]).astype(BF16), LONG_UP)
    in_opposite = in_piece(6, 2, grad_scale, BF16)
    grads_other, *grads = row_part(clock(preact_grad), in_full, 0)
    clock.step(in_opposite, grads_other, out_through, out_near, layer_through, layer_near)
    grads_swap = send(clock(grads_other), SWAP)
    in_through = send(clock(in_opposite), Z_BACK)
    layer_third = add(*layer[1], clock(layer_through)).astype(BF16)
    layer_far = send(layer_third, LONG_DOWN)
    out_third = out_piece(2, 2, grad_scale, BF16, clock(out_through))
    out_last = send(out_third, Z_BACK)
    clock.step(out_third, layer_third, grads_swap)
    grads = list(zip(grads, parts(clock(grads_swap))))
    grads_3, grads_1 = add(*grads[3]).astype(BF16), add(*grads[1]).astype(BF16)
    grads_through, grads_near = send(grads_3, LONG_UP), send(grads_1, LONG_DOWN)
    in_beside = [in_piece(4 + j, 1, grad_scale, BF16) for j in range(2)]
    clock.step(*in_beside, grads_1, grads_3, layer_far, in_through, out_last, grads_through, grads_near)
    in_near = [send(clock(v), Z_AHEAD) for v in in_beside]
    in_through = clock(in_through)
    in_third = [in_piece(2 + j, 1, grad_scale, BF16, in_through[j : j + 1]) for j in range(2)]
    in_last_1 = send(in_third[1], Z_BACK)
    grads_third = add(*grads[2], clock(grads_through)).astype(BF16)
    grads_far = send(grads_third, LONG_UP)
    out_sum = out_piece(0, 2, grad_scale, F32, out_near, out_last)
    out_there = send(out_sum[1].astype(BF16), PAIR)
    layer_sum = add(*layer[0], layer_near, clock(layer_far))
    clock.step(*in_third, layer_sum, grads_far, *in_near, in_last_1, out_there)
    in_last_0 = send(clock(in_third[0]), Z_BACK)
    in_there = in_piece(1, 1, grad_scale, BF16, clock(in_near[1]), clock(in_last_1))[0]
    in_there = send(in_there, PAIR)
    sums = jnp.stack([clock(layer_sum), add(*grads[0], grads_near, clock(grads_far))])

    def beside(here, there, axis):
        there = there.astype(F32)
        return jnp.concatenate(
            [jnp.where(x_lo == 0, here, there), jnp.where(x_lo == 0, there, here)], axis
        )

    sums = sums.reshape(2, 4, rows, -1)
    up = send(sums[:, 2].astype(BF16), SHORT_UP)
    down = send(sums[:, 1].astype(BF16), SHORT_DOWN)
    far = send(sums[:, 3].astype(BF16), SHORT_FAR)
    clock.step(up, down, far, in_last_0)
    in_here = in_piece(0, 1, grad_scale, F32, clock(in_near[0]), clock(in_last_0))[0]
    total = add(sums[:, 0], clock(up), clock(down), clock(far)).astype(BF16)

    return (
        total[0],
        total[1],
        beside(in_here, in_there, 1),
        beside(out_sum[0], out_there, 0),
    )


def solution(mesh):
    return jax.shard_map(
        local,
        mesh=mesh,
        in_specs=(
            P(("dp", "tensor"), None),
            P("dp", "tensor"),
            P("tensor", "dp"),
            P(("dp", "tensor"), None),
        ),
        out_specs=(
            P(("dp", "tensor"), None),
            P(("dp", "tensor"), None),
            P("dp", "tensor"),
            P("tensor", "dp"),
        ),
        check_vma=False,
    )
```

```python
import functools
import math

import jax
import jax.numpy as jnp
from jax import lax
from jax.experimental import pallas as pl
from jax.experimental.pallas import tpu as pltpu
from jax.sharding import PartitionSpec as P

AXES = ("dp", "tensor")
F32, BF16 = jnp.float32, jnp.bfloat16
TILE = 512


def index_of(x, y, z, core):
    return ((x % 2 * 4 + z) * 2 + x // 2) * 8 + y * 2 + core


def route(step):
    pairs = []
    for x in range(4):
        for y in range(4):
            for z in range(4):
                for core in range(2):
                    tx, ty, tz, tc = step(x, y, z, core)
                    pairs.append((index_of(x, y, z, core), index_of(tx % 4, ty % 4, tz % 4, tc)))
    return pairs


def way(core):
    return 1 - 2 * core


def along(hop, first):
    return route(lambda x, y, z, c: (x + hop, y, z, c) if c == first else (x, y + hop, z, c))


Z_AHEAD = route(lambda x, y, z, c: (x, y, z + way(c), c))
Z_BACK = route(lambda x, y, z, c: (x, y, z - way(c), c))
LONG_UP, LONG_DOWN = along(1, 0), along(-1, 0)
SHORT_UP, SHORT_DOWN, SHORT_FAR = along(1, 1), along(-1, 1), along(2, 1)
PAIR = route(lambda x, y, z, c: (x ^ 1, y, z, c))
Z_BACK_PAIR = route(lambda x, y, z, c: (x ^ 1, y, z - way(c), c))
SWAP = route(lambda x, y, z, c: (x, y, z, 1 - c))


def send(value, pairs):
    return lax.ppermute(value, AXES, pairs)


def after(value, *others):
    return lax.optimization_barrier((value, others))[0]


def marker_body(value, out):
    out[...] = value[...]


def marker(*others):
    return pl.pallas_call(
        marker_body,
        out_shape=jax.ShapeDtypeStruct((8, 128), F32),
        cost_estimate=pl.CostEstimate(flops=1, bytes_accessed=1, transcendentals=0),
    )(after(jnp.zeros((8, 128), F32), *others))


class Clock:
    def __init__(self):
        self.token, self.waits = jnp.zeros((8, 128), F32), ()

    def step(self, *waits):
        if self.waits is not None:
            self.token = marker(self.token, *self.waits)
        self.waits = waits

    def __call__(self, value):
        return after(value, self.token, *self.waits)


def add(*terms):
    return sum(t.astype(F32) for t in terms)


def gelu_and_slope(value):
    cdf = 0.5 * (1.0 + lax.erf(value / math.sqrt(2.0)))
    slope = cdf + value * jnp.exp(-0.5 * value * value) / math.sqrt(2.0 * math.pi)
    return value * cdf, slope


def dot(left, right, dims):
    return lax.dot_general(left, right, (dims, ((), ())), preferred_element_type=F32)


def params():
    return pltpu.CompilerParams(vmem_limit_bytes=14 << 20)


def cost(rows, depth, columns):
    return pl.CostEstimate(flops=1, bytes_accessed=1, transcendentals=0)


def weight_part_body(scale, table, left, right, *rest):
    total = dot(left[...], right[...], ((0,), (0,))) * scale
    for term in rest[:-1]:
        total += term[...].reshape(total.shape).astype(F32)
    rest[-1][...] = total.astype(rest[-1].dtype).reshape(rest[-1].shape)


def weight_part(table, left, right, pick, first, count, scale, kind, *terms):
    rows = left.shape[0]
    whole = pl.BlockSpec((rows, TILE), lambda j, t: (0, 0))
    block = pl.BlockSpec((rows, TILE), lambda j, t: (0, t[first + j]))
    tile = pl.BlockSpec((1, TILE, TILE), lambda j, t: (j, 0, 0))
    return pl.pallas_call(
        functools.partial(weight_part_body, scale),
        grid_spec=pltpu.PrefetchScalarGridSpec(
            num_scalar_prefetch=1,
            grid=(count,),
            in_specs=[block, whole][:: 1 if pick == 0 else -1] + [tile] * len(terms),
            out_specs=tile,
        ),
        out_shape=jax.ShapeDtypeStruct((count, TILE, TILE), kind),
        compiler_params=params(),
        cost_estimate=cost(TILE, rows, count * TILE),
    )(table, left, right, *terms)


def row_part_body(dims, left, right, other, *own):
    total = dot(left[...], right[...], dims)
    size = own[0].shape[0]
    for i, out in enumerate(own):
        out[...] = total[i * size : (i + 1) * size].astype(BF16)
    other[...] = total[len(own) * size :].astype(BF16)


def row_part(left, right, axis):
    rows, width, tile = left.shape[0], right.shape[axis], 2 * TILE
    weight = pl.BlockSpec((TILE, tile), lambda n: (0, n)) if axis else pl.BlockSpec((tile, TILE), lambda n: (n, 0))
    sizes = [rows // 2] + [rows // 8] * 4
    return pl.pallas_call(
        functools.partial(row_part_body, ((1,), (1 - axis,))),
        grid=(width // tile,),
        in_specs=[pl.BlockSpec((rows, TILE), lambda n: (0, 0)), weight],
        out_specs=[pl.BlockSpec((size, tile), lambda n: (0, n)) for size in sizes],
        out_shape=[jax.ShapeDtypeStruct((size, width), BF16) for size in sizes],
        compiler_params=pltpu.CompilerParams(vmem_limit_bytes=24 << 20),
        cost_estimate=cost(rows, TILE, width),
    )(left, right)


def preact_grad_body(left, right, slope, out, total):
    step = pl.program_id(0)
    product = dot(left[...], right[...], ((1,), (1,)))

    @pl.when(step == 0)
    def _():
        total[...] = product

    @pl.when(step > 0)
    def _():
        total[...] += product

    @pl.when(step == pl.num_programs(0) - 1)
    def _():
        out[...] = (total[...] * slope[...]).astype(BF16)


def preact_grad_of(left, right, slope):
    rows, width, tile = left.shape[0], left.shape[1], 2 * TILE
    whole = pl.BlockSpec((rows, TILE), lambda k: (0, 0))
    return pl.pallas_call(
        preact_grad_body,
        grid=(width // tile,),
        in_specs=[pl.BlockSpec((rows, tile), lambda k: (0, k)), pl.BlockSpec((TILE, tile), lambda k: (0, k)), whole],
        out_specs=whole,
        out_shape=jax.ShapeDtypeStruct((rows, TILE), BF16),
        scratch_shapes=[pltpu.VMEM((rows, TILE), F32)],
        compiler_params=pltpu.CompilerParams(vmem_limit_bytes=24 << 20),
        cost_estimate=cost(rows, TILE, width),
    )(left, right, slope)


def local(tokens, w_in, w_out, out_grad):
    dp, tensor = lax.axis_index("dp"), lax.axis_index("tensor")
    x_lo, z, core = dp // 4, dp % 4, tensor % 2
    side = 1 - 2 * core
    rows = tokens.shape[0]
    grad_scale = 1.0 / math.sqrt(rows * 128)

    ring = [z, (z - side) % 4, (z + side) % 4, (z + 2) % 4]
    places = [a * 4 + b for a in (x_lo, 1 - x_lo) for b in ring]
    table = jnp.stack(places).astype(jnp.int32)
    part_table = table.reshape(2, 4).T.reshape(8)

    def halves(value, axis):
        mine = lax.dynamic_slice_in_dim(value, x_lo * TILE, TILE, axis)
        other = lax.dynamic_slice_in_dim(value, (1 - x_lo) * TILE, TILE, axis)
        return mine, other

    in_mine, in_other = halves(w_in, 1)
    out_mine, out_other = halves(w_out, 0)
    both = jnp.stack([tokens, out_grad])

    clock = Clock()
    in_a_behind, in_a_ahead = send(in_mine, Z_AHEAD), send(in_mine, Z_BACK)
    pair = send(jnp.stack([in_other, out_other]), PAIR)
    clock.step()
    short_up, short_down = send(clock(both), SHORT_UP), send(clock(both), SHORT_DOWN)
    clock.step(in_a_behind, in_a_ahead)
    in_a_far = send(clock(in_a_behind), Z_AHEAD)
    short_far = send(clock(both), SHORT_FAR)
    clock.step(short_far, in_a_far, pair)
    in_pair, out_pair = clock(pair[0]), clock(pair[1])
    start_in, start_out = clock(jnp.zeros((8 * TILE, TILE), BF16)), clock(jnp.zeros((TILE, 8 * TILE), BF16))
    rows_own = clock(jnp.concatenate([both, short_up, short_down, short_far], 1))
    rows_up, rows_down = send(rows_own, LONG_UP), send(rows_own, LONG_DOWN)
    rows_own_swap = send(rows_own, SWAP)
    in_b_behind, in_b_ahead = send(in_pair, Z_AHEAD), send(in_pair, Z_BACK)
    clock.step(rows_own_swap)
    out_own = clock(jnp.stack([out_mine, out_pair]))
    out_behind = send(out_own, Z_AHEAD)
    clock.step(rows_up, rows_down, in_b_behind, in_b_ahead, out_behind)
    rows_up, rows_down = clock(rows_up), clock(rows_down)
    tok_far, cot_far = send(rows_up[0], LONG_UP), send(rows_down[1], LONG_DOWN)
    rows_up_swap, rows_down_swap = send(rows_up, SWAP), send(rows_down, SWAP)
    out_ahead = send(clock(out_own), Z_BACK)
    clock.step(rows_up_swap, rows_down_swap)
    clock.step(tok_far, cot_far, out_ahead)
    tok_far_swap, cot_far_swap = send(clock(tok_far), SWAP), send(clock(cot_far), SWAP)
    in_b_far = send(clock(in_b_behind), Z_AHEAD)
    out_far = send(clock(out_behind), Z_AHEAD)
    clock.step(tok_far_swap, cot_far_swap, in_b_far)

    in_full = start_in
    for i, piece in enumerate([in_mine, in_a_behind, in_a_ahead, in_a_far, in_pair, in_b_behind, in_b_ahead, in_b_far]):
        in_full = lax.dynamic_update_slice(in_full, piece, (places[i] * TILE, 0))
    out_full = start_out

    def placed(full, i, pieces):
        for j in range(2):
            full = lax.dynamic_update_slice(full, pieces[j], (0, places[i + 4 * j] * TILE))
        return full

    for i, pieces in enumerate((out_own, out_behind)):
        out_full = placed(out_full, i, pieces)
    def whole(which, far, far_swap):
        near = [rows_own[which], rows_up[which], rows_down[which], far]
        swap = [rows_own_swap[which], rows_up_swap[which], rows_down_swap[which], far_swap]
        return jnp.concatenate(near + swap, 0)

    token_rows = clock(whole(0, tok_far, tok_far_swap))
    cotan_rows = whole(1, cot_far, cot_far_swap)

    preact = dot(token_rows, in_full, ((1,), (0,)))
    hidden, slope = gelu_and_slope(preact)
    hidden = hidden.astype(BF16)


    def out_piece(*rest):
        return weight_part(part_table, clock(hidden), cotan_rows, 1, *rest)

    def in_piece(*rest):
        return weight_part(part_table, token_rows, clock(preact_grad), 0, *rest)

    clock.step(hidden)
    out_opposite = out_piece(6, 2, grad_scale, BF16)
    out_through = send(out_opposite, Z_BACK)
    out_beside = out_piece(4, 2, grad_scale, BF16)
    out_near = send(out_beside, Z_AHEAD)
    clock.step(out_ahead, out_opposite, out_beside)
    out_full = placed(out_full, 2, clock(out_ahead))
    clock.step(out_far, out_full)
    out_full = placed(clock(out_full), 3, clock(out_far))
    layer_other, *layer = row_part(clock(hidden), out_full, 1)
    clock.step(layer_other)
    layer_swap = send(clock(layer_other), SWAP)
    preact_grad = preact_grad_of(cotan_rows, clock(out_full), slope)
    clock.step(preact_grad, layer_swap)

    def parts(value):
        return [value[i : i + 4 * rows] for i in range(0, 16 * rows, 4 * rows)]

    layer = list(zip(layer, parts(clock(layer_swap))))
    layer_through = send(add(*layer[3]).astype(BF16), LONG_DOWN)
    layer_near = send(add(*layer[2]).astype(BF16), LONG_UP)
    in_opposite = in_piece(6, 2, grad_scale, BF16)
    grads_other, *grads = row_part(clock(preact_grad), in_full, 0)
    clock.step(in_opposite, grads_other, out_through, out_near, layer_through, layer_near)
    grads_swap = send(clock(grads_other), SWAP)
    in_through = send(clock(in_opposite), Z_BACK)
    layer_third = add(*layer[1], clock(layer_through)).astype(BF16)
    layer_far = send(layer_third, LONG_DOWN)
    out_third = out_piece(2, 2, grad_scale, BF16, clock(out_through))
    out_last = send(out_third, Z_BACK)
    clock.step(out_third, layer_third, grads_swap)
    grads = list(zip(grads, parts(clock(grads_swap))))
    grads_3, grads_1 = add(*grads[3]).astype(BF16), add(*grads[1]).astype(BF16)
    grads_through, grads_near = send(grads_3, LONG_UP), send(grads_1, LONG_DOWN)
    in_beside = [in_piece(4 + j, 1, grad_scale, BF16) for j in range(2)]
    clock.step(*in_beside, grads_1, grads_3, layer_far, in_through, out_last, grads_through, grads_near)
    in_near = [send(clock(v), Z_AHEAD) for v in in_beside]
    in_through = clock(in_through)
    in_third = [in_piece(2 + j, 1, grad_scale, BF16, in_through[j : j + 1]) for j in range(2)]
    in_last_1 = send(in_third[1], Z_BACK)
    grads_third = add(*grads[2], clock(grads_through)).astype(BF16)
    grads_far = send(grads_third, LONG_UP)
    out_sum = out_piece(0, 2, grad_scale, F32, out_near, out_last)
    out_there = send(out_sum[1].astype(BF16), PAIR)
    layer_sum = add(*layer[0], layer_near, clock(layer_far))
    clock.step(*in_third, layer_sum, grads_far, *in_near, in_last_1, out_there)
    in_last_0 = send(clock(in_third[0]), Z_BACK)
    in_there = in_piece(1, 1, grad_scale, BF16, clock(in_near[1]), clock(in_last_1))[0]
    in_there = send(in_there, PAIR)
    sums = jnp.stack([clock(layer_sum), add(*grads[0], grads_near, clock(grads_far))])

    def beside(here, there, axis):
        there = there.astype(F32)
        return jnp.concatenate(
            [jnp.where(x_lo == 0, here, there), jnp.where(x_lo == 0, there, here)], axis
        )

    sums = sums.reshape(2, 4, rows, -1)
    up = send(sums[:, 2].astype(BF16), SHORT_UP)
    down = send(sums[:, 1].astype(BF16), SHORT_DOWN)
    far = send(sums[:, 3].astype(BF16), SHORT_FAR)
    clock.step(up, down, far, in_last_0)
    in_here = in_piece(0, 1, grad_scale, F32, clock(in_near[0]), clock(in_last_0))[0]
    total = add(sums[:, 0], clock(up), clock(down), clock(far)).astype(BF16)

    return (
        total[0],
        total[1],
        beside(in_here, in_there, 1),
        beside(out_sum[0], out_there, 0),
    )


def solution(mesh):
    return jax.shard_map(
        local,
        mesh=mesh,
        in_specs=(
            P(("dp", "tensor"), None),
            P("dp", "tensor"),
            P("tensor", "dp"),
            P(("dp", "tensor"), None),
        ),
        out_specs=(
            P(("dp", "tensor"), None),
            P(("dp", "tensor"), None),
            P("dp", "tensor"),
            P("tensor", "dp"),
        ),
        check_vma=False,
    )
```

```python
import functools
import math

import jax
import jax.numpy as jnp
from jax import lax
from jax.experimental import pallas as pl
from jax.experimental.pallas import tpu as pltpu
from jax.sharding import PartitionSpec as P

AXES = ("dp", "tensor")
F32, BF16 = jnp.float32, jnp.bfloat16
TILE = 512


def index_of(x, y, z, core):
    return ((x % 2 * 4 + z) * 2 + x // 2) * 8 + y * 2 + core


def route(step):
    pairs = []
    for x in range(4):
        for y in range(4):
            for z in range(4):
                for core in range(2):
                    tx, ty, tz, tc = step(x, y, z, core)
                    pairs.append((index_of(x, y, z, core), index_of(tx % 4, ty % 4, tz % 4, tc)))
    return pairs


def way(core):
    return 1 - 2 * core


def along(hop, first):
    return route(lambda x, y, z, c: (x + hop, y, z, c) if c == first else (x, y + hop, z, c))


Z_AHEAD = route(lambda x, y, z, c: (x, y, z + way(c), c))
Z_BACK = route(lambda x, y, z, c: (x, y, z - way(c), c))
LONG_UP, LONG_DOWN = along(1, 0), along(-1, 0)
SHORT_UP, SHORT_DOWN, SHORT_FAR = along(1, 1), along(-1, 1), along(2, 1)
PAIR = route(lambda x, y, z, c: (x ^ 1, y, z, c))
Z_BACK_PAIR = route(lambda x, y, z, c: (x ^ 1, y, z - way(c), c))
SWAP = route(lambda x, y, z, c: (x, y, z, 1 - c))


def send(value, pairs):
    return lax.ppermute(value, AXES, pairs)


def after(value, *others):
    return lax.optimization_barrier((value, others))[0]


def marker_body(value, out):
    out[...] = value[...]


def marker(*others):
    return pl.pallas_call(
        marker_body,
        out_shape=jax.ShapeDtypeStruct((8, 128), F32),
        cost_estimate=pl.CostEstimate(flops=1, bytes_accessed=1, transcendentals=0),
    )(after(jnp.zeros((8, 128), F32), *others))


class Clock:
    def __init__(self):
        self.token, self.waits = jnp.zeros((8, 128), F32), ()

    def step(self, *waits):
        if self.waits is not None:
            self.token = marker(self.token, *self.waits)
        self.waits = waits

    def __call__(self, value):
        return after(value, self.token, *self.waits)


def add(*terms):
    return sum(t.astype(F32) for t in terms)


def gelu_and_slope(value):
    cdf = 0.5 * (1.0 + lax.erf(value / math.sqrt(2.0)))
    slope = cdf + value * jnp.exp(-0.5 * value * value) / math.sqrt(2.0 * math.pi)
    return value * cdf, slope


def dot(left, right, dims):
    return lax.dot_general(left, right, (dims, ((), ())), preferred_element_type=F32)


def params():
    return pltpu.CompilerParams(vmem_limit_bytes=14 << 20)


def cost(rows, depth, columns):
    return pl.CostEstimate(flops=1, bytes_accessed=1, transcendentals=0)


def weight_part_body(scale, table, left, right, *rest):
    total = dot(left[...], right[...], ((0,), (0,))) * scale
    for term in rest[:-1]:
        total += term[...].reshape(total.shape).astype(F32)
    rest[-1][...] = total.astype(rest[-1].dtype).reshape(rest[-1].shape)


def weight_part(table, left, right, pick, first, count, scale, kind, *terms):
    rows = left.shape[0]
    whole = pl.BlockSpec((rows, TILE), lambda j, t: (0, 0))
    block = pl.BlockSpec((rows, TILE), lambda j, t: (0, t[first + j]))
    tile = pl.BlockSpec((1, TILE, TILE), lambda j, t: (j, 0, 0))
    return pl.pallas_call(
        functools.partial(weight_part_body, scale),
        grid_spec=pltpu.PrefetchScalarGridSpec(
            num_scalar_prefetch=1,
            grid=(count,),
            in_specs=[block, whole][:: 1 if pick == 0 else -1] + [tile] * len(terms),
            out_specs=tile,
        ),
        out_shape=jax.ShapeDtypeStruct((count, TILE, TILE), kind),
        compiler_params=params(),
        cost_estimate=cost(TILE, rows, count * TILE),
    )(table, left, right, *terms)


def row_part_body(dims, left, right, other, *own):
    total = dot(left[...], right[...], dims)
    size = own[0].shape[0]
    for i, out in enumerate(own):
        out[...] = total[i * size : (i + 1) * size].astype(BF16)
    other[...] = total[len(own) * size :].astype(BF16)


def row_part(left, right, axis):
    rows, width, tile = left.shape[0], right.shape[axis], 2 * TILE
    weight = pl.BlockSpec((TILE, tile), lambda n: (0, n)) if axis else pl.BlockSpec((tile, TILE), lambda n: (n, 0))
    sizes = [rows // 2] + [rows // 8] * 4
    return pl.pallas_call(
        functools.partial(row_part_body, ((1,), (1 - axis,))),
        grid=(width // tile,),
        in_specs=[pl.BlockSpec((rows, TILE), lambda n: (0, 0)), weight],
        out_specs=[pl.BlockSpec((size, tile), lambda n: (0, n)) for size in sizes],
        out_shape=[jax.ShapeDtypeStruct((size, width), BF16) for size in sizes],
        compiler_params=pltpu.CompilerParams(vmem_limit_bytes=24 << 20),
        cost_estimate=cost(rows, TILE, width),
    )(left, right)


def preact_grad_body(left, right, slope, out, total):
    step = pl.program_id(0)
    product = dot(left[...], right[...], ((1,), (1,)))

    @pl.when(step == 0)
    def _():
        total[...] = product

    @pl.when(step > 0)
    def _():
        total[...] += product

    @pl.when(step == pl.num_programs(0) - 1)
    def _():
        out[...] = (total[...] * slope[...]).astype(BF16)


def preact_grad_of(left, right, slope):
    rows, width, tile = left.shape[0], left.shape[1], 2 * TILE
    whole = pl.BlockSpec((rows, TILE), lambda k: (0, 0))
    return pl.pallas_call(
        preact_grad_body,
        grid=(width // tile,),
        in_specs=[pl.BlockSpec((rows, tile), lambda k: (0, k)), pl.BlockSpec((TILE, tile), lambda k: (0, k)), whole],
        out_specs=whole,
        out_shape=jax.ShapeDtypeStruct((rows, TILE), BF16),
        scratch_shapes=[pltpu.VMEM((rows, TILE), F32)],
        compiler_params=pltpu.CompilerParams(vmem_limit_bytes=24 << 20),
        cost_estimate=cost(rows, TILE, width),
    )(left, right, slope)


def local(tokens, w_in, w_out, out_grad):
    dp, tensor = lax.axis_index("dp"), lax.axis_index("tensor")
    x_lo, z, core = dp // 4, dp % 4, tensor % 2
    side = 1 - 2 * core
    rows = tokens.shape[0]
    grad_scale = 1.0 / math.sqrt(rows * 128)

    ring = [z, (z - side) % 4, (z + side) % 4, (z + 2) % 4]
    places = [a * 4 + b for a in (x_lo, 1 - x_lo) for b in ring]
    table = jnp.stack(places).astype(jnp.int32)
    part_table = table.reshape(2, 4).T.reshape(8)

    def halves(value, axis):
        mine = lax.dynamic_slice_in_dim(value, x_lo * TILE, TILE, axis)
        other = lax.dynamic_slice_in_dim(value, (1 - x_lo) * TILE, TILE, axis)
        return mine, other

    in_mine, in_other = halves(w_in, 1)
    out_mine, out_other = halves(w_out, 0)
    both = jnp.stack([tokens, out_grad])

    clock = Clock()
    in_a_behind, in_a_ahead = send(in_mine, Z_AHEAD), send(in_mine, Z_BACK)
    clock.step()
    short_up, short_down = send(clock(both), SHORT_UP), send(clock(both), SHORT_DOWN)
    clock.step()
    pair = send(clock(jnp.stack([in_other, out_other])), PAIR)
    clock.step(in_a_behind, in_a_ahead)
    in_a_far = send(clock(in_a_behind), Z_AHEAD)
    short_far = send(clock(both), SHORT_FAR)
    clock.step(short_far, in_a_far, pair)
    in_pair, out_pair = clock(pair[0]), clock(pair[1])
    start_in, start_out = clock(jnp.zeros((8 * TILE, TILE), BF16)), clock(jnp.zeros((TILE, 8 * TILE), BF16))
    rows_own = clock(jnp.concatenate([both, short_up, short_down, short_far], 1))
    rows_up, rows_down = send(rows_own, LONG_UP), send(rows_own, LONG_DOWN)
    rows_own_swap = send(rows_own, SWAP)
    in_b_behind, in_b_ahead = send(in_pair, Z_AHEAD), send(in_pair, Z_BACK)
    clock.step(rows_own_swap)
    out_own = clock(jnp.stack([out_mine, out_pair]))
    out_behind = send(out_own, Z_AHEAD)
    clock.step(rows_up, rows_down, in_b_behind, in_b_ahead, out_behind)
    rows_up, rows_down = clock(rows_up), clock(rows_down)
    tok_far, cot_far = send(rows_up[0], LONG_UP), send(rows_down[1], LONG_DOWN)
    rows_up_swap, rows_down_swap = send(rows_up, SWAP), send(rows_down, SWAP)
    out_ahead = send(clock(out_own), Z_BACK)
    clock.step(rows_up_swap, rows_down_swap)
    clock.step(tok_far, cot_far, out_ahead)
    tok_far_swap, cot_far_swap = send(clock(tok_far), SWAP), send(clock(cot_far), SWAP)
    in_b_far = send(clock(in_b_behind), Z_AHEAD)
    out_far = send(clock(out_behind), Z_AHEAD)
    clock.step(tok_far_swap, cot_far_swap, in_b_far)

    in_full = start_in
    for i, piece in enumerate([in_mine, in_a_behind, in_a_ahead, in_a_far, in_pair, in_b_behind, in_b_ahead, in_b_far]):
        in_full = lax.dynamic_update_slice(in_full, piece, (places[i] * TILE, 0))
    out_full = start_out

    def placed(full, i, pieces):
        for j in range(2):
            full = lax.dynamic_update_slice(full, pieces[j], (0, places[i + 4 * j] * TILE))
        return full

    for i, pieces in enumerate((out_own, out_behind)):
        out_full = placed(out_full, i, pieces)
    def whole(which, far, far_swap):
        near = [rows_own[which], rows_up[which], rows_down[which], far]
        swap = [rows_own_swap[which], rows_up_swap[which], rows_down_swap[which], far_swap]
        return jnp.concatenate(near + swap, 0)

    token_rows = clock(whole(0, tok_far, tok_far_swap))
    cotan_rows = whole(1, cot_far, cot_far_swap)

    preact = dot(token_rows, in_full, ((1,), (0,)))
    hidden, slope = gelu_and_slope(preact)
    hidden = hidden.astype(BF16)


    def out_piece(*rest):
        return weight_part(part_table, clock(hidden), cotan_rows, 1, *rest)

    def in_piece(*rest):
        return weight_part(part_table, token_rows, clock(preact_grad), 0, *rest)

    clock.step(hidden)
    out_opposite = out_piece(6, 2, grad_scale, BF16)
    out_through = send(out_opposite, Z_BACK)
    out_beside = out_piece(4, 2, grad_scale, BF16)
    out_near = send(out_beside, Z_AHEAD)
    clock.step(out_ahead, out_opposite, out_beside)
    out_full = placed(out_full, 2, clock(out_ahead))
    clock.step(out_far, out_full)
    out_full = placed(clock(out_full), 3, clock(out_far))
    layer_other, *layer = row_part(clock(hidden), out_full, 1)
    clock.step(layer_other)
    layer_swap = send(clock(layer_other), SWAP)
    preact_grad = preact_grad_of(cotan_rows, clock(out_full), slope)
    clock.step(preact_grad, layer_swap)

    def parts(value):
        return [value[i : i + 4 * rows] for i in range(0, 16 * rows, 4 * rows)]

    layer = list(zip(layer, parts(clock(layer_swap))))
    layer_through = send(add(*layer[3]).astype(BF16), LONG_DOWN)
    layer_near = send(add(*layer[2]).astype(BF16), LONG_UP)
    in_opposite = in_piece(6, 2, grad_scale, BF16)
    grads_other, *grads = row_part(clock(preact_grad), in_full, 0)
    clock.step(in_opposite, grads_other, out_through, out_near, layer_through, layer_near)
    grads_swap = send(clock(grads_other), SWAP)
    in_through = send(clock(in_opposite), Z_BACK)
    layer_third = add(*layer[1], clock(layer_through)).astype(BF16)
    layer_far = send(layer_third, LONG_DOWN)
    out_third = out_piece(2, 2, grad_scale, BF16, clock(out_through))
    out_last = send(out_third, Z_BACK)
    clock.step(out_third, layer_third, grads_swap)
    grads = list(zip(grads, parts(clock(grads_swap))))
    grads_3, grads_1 = add(*grads[3]).astype(BF16), add(*grads[1]).astype(BF16)
    grads_through, grads_near = send(grads_3, LONG_UP), send(grads_1, LONG_DOWN)
    in_beside = [in_piece(4 + j, 1, grad_scale, BF16) for j in range(2)]
    clock.step(*in_beside, grads_1, grads_3, layer_far, in_through, out_last, grads_through, grads_near)
    in_near = [send(clock(v), Z_AHEAD) for v in in_beside]
    in_through = clock(in_through)
    in_third = [in_piece(2 + j, 1, grad_scale, BF16, in_through[j : j + 1]) for j in range(2)]
    in_last_1 = send(in_third[1], Z_BACK)
    grads_third = add(*grads[2], clock(grads_through)).astype(BF16)
    grads_far = send(grads_third, LONG_UP)
    out_sum = out_piece(0, 2, grad_scale, F32, out_near, out_last)
    out_there = send(out_sum[1].astype(BF16), PAIR)
    layer_sum = add(*layer[0], layer_near, clock(layer_far))
    clock.step(*in_third, layer_sum, grads_far, *in_near, in_last_1, out_there)
    in_last_0 = send(clock(in_third[0]), Z_BACK)
    in_there = in_piece(1, 1, grad_scale, BF16, clock(in_near[1]), clock(in_last_1))[0]
    in_there = send(in_there, PAIR)
    sums = jnp.stack([clock(layer_sum), add(*grads[0], grads_near, clock(grads_far))])

    def beside(here, there, axis):
        there = there.astype(F32)
        return jnp.concatenate(
            [jnp.where(x_lo == 0, here, there), jnp.where(x_lo == 0, there, here)], axis
        )

    sums = sums.reshape(2, 4, rows, -1)
    up = send(sums[:, 2].astype(BF16), SHORT_UP)
    down = send(sums[:, 1].astype(BF16), SHORT_DOWN)
    far = send(sums[:, 3].astype(BF16), SHORT_FAR)
    clock.step(up, down, far, in_last_0)
    in_here = in_piece(0, 1, grad_scale, F32, clock(in_near[0]), clock(in_last_0))[0]
    total = add(sums[:, 0], clock(up), clock(down), clock(far)).astype(BF16)

    return (
        total[0],
        total[1],
        beside(in_here, in_there, 1),
        beside(out_sum[0], out_there, 0),
    )


def solution(mesh):
    return jax.shard_map(
        local,
        mesh=mesh,
        in_specs=(
            P(("dp", "tensor"), None),
            P("dp", "tensor"),
            P("tensor", "dp"),
            P(("dp", "tensor"), None),
        ),
        out_specs=(
            P(("dp", "tensor"), None),
            P(("dp", "tensor"), None),
            P("dp", "tensor"),
            P("tensor", "dp"),
        ),
        check_vma=False,
    )
```
